32 devices in a mesh: group: 1, expert: 16 (over z, y, x), step: 2 (over core).
Axes of the slice: x: 2, y: 2, z: 4, core: 2. Of those that a mesh axis runs over, the one named last changes fastest.
Arguments:
- latents: float32 [2, 2048, 1536], P('step', ('group', 'expert')), may hold values from -6 to 6
- modulation: float32 [2, 6, 1536], P('group'), may hold values from -3 to 3
- shallow_routes: int32 [2, 2048, 2], P('step', ('group', 'expert')), may hold values from 0 to 3, all different within a row; in each aligned block of 128 rows (0 to 127, 128 to 255, ..., all dimensions but the last counted through in order) at most 64 rows name the same one
- deep_routes: int32 [2048, 2], P(('group', 'expert')), may hold values from 0 to 3, all different within a row; in each aligned block of 128 rows (0 to 127, 128 to 255, ...) at most 64 rows name the same one
- refresh: int32 [16], P(('group', 'expert')), may hold values from 0 to 1
- shallow_in: bfloat16 [16, 1536, 768], P('expert'), may hold values from -0.15625 to 0.15625
- shallow_out: bfloat16 [16, 768, 1536], P('expert'), may hold values from -0.109375 to 0.109375
- deep_in: bfloat16 [16, 1536, 768], P('expert'), may hold values from -0.15625 to 0.15625
- deep_out: bfloat16 [16, 768, 1536], P('expert'), may hold values from -0.109375 to 0.109375
- shallow_router: float32 [1536, 4], replicated, may hold values from -0.15625 to 0.15625
- deep_router: float32 [1536, 4], replicated, may hold values from -0.15625 to 0.15625
Outputs:
- result: bfloat16 [2, 2048, 1536], P('step', ('group', 'expert'))
The draws below stay inside these ranges and needn't reach their ends.
Inputs may be any that keep to these rules, and one draw needn't show every extreme that they name: `shallow_routes`: within the 128 rows of one index of expert (aligned blocks), each expert is named by at most 64 rows, and by exactly 64 rows in some block; a row names two different experts. `deep_routes`: within the 128 rows of one index of expert (aligned blocks), each expert is named by at most 64 rows, and by exactly 64 rows in some block; a row names two different experts.
All inputs are finite; a program needn't handle non-finite values.
Results may differ from the reference program's by a relative error of at most 0.01.
Values may be sent and summed in bfloat16 or wider, within the bound.
A program may use at most 64 MiB of HBM per device.

```python
import math
import jax
import jax.numpy as jnp
import numpy as np
from jax import lax

D = 1536
FF = 3072
QUARTERS = 4
TOK_DEV = 128
EXPERTS = 4
FF_DEV = 768
CAP = 64
TOKENS = 2048
N_EXPERT = 16


def with_ends(result, rng, smallest, largest):
    place = [jax.random.randint(jax.random.fold_in(rng, axis), (), 0, length) for axis, length in enumerate(result.shape)]
    main_axis = result.shape.index(max(result.shape))
    beside = place[:main_axis] + [(place[main_axis] + 1) % result.shape[main_axis]] + place[main_axis + 1:]
    return result.at[tuple(place)].set(smallest).at[tuple(beside)].set(largest)


def block_levels(rng, shape, shards, low, largest):
    factor_of = 1.0
    for dim, parts in shards:
        steps = jax.random.uniform(jax.random.fold_in(jax.random.fold_in(rng, 6), dim), (parts,), jnp.float32, low / len(shards), largest / len(shards))
        factor_of = factor_of * jnp.repeat(jnp.exp(steps), shape[dim] // parts).reshape((-1,) + (1,) * (len(shape) - 1 - dim))
    return factor_of


def routed_block(own_key, own, number, rows, amount, top, reach, lean):
    sequence = jax.random.permutation(own_key, amount)
    heavy_load, ordinary = shares(amount, rows * top, reach, lean, True), shares(amount, rows * top, reach, lean, False)
    places = jnp.arange(amount)

    def named(tallies, rotation):
        used = int((tallies > 0).sum())
        fixed = max(1, used // 4)
        shifted = fixed + (places - fixed + rotation * (used - fixed)) % max(1, amount - fixed)
        return jnp.zeros((amount,), jnp.int32).at[sequence[jnp.where(places < fixed, places, shifted)]].set(jnp.asarray(tallies, jnp.int32))

    tallies = jnp.where(number % 4 == 0, named(heavy_load, number // 4), named(ordinary, number - number // 4 - 1))
    mixed = jax.random.permutation(jax.random.fold_in(own, 3), amount)
    donor, receiver = mixed[0:amount // 2 * 2:2], mixed[1:amount // 2 * 2:2]
    slack = jnp.minimum(tallies[donor] - 1, reach - tallies[receiver]) // 2
    slack = jnp.where((donor == sequence[0]) | (receiver == sequence[0]) | (tallies[receiver] == 0), 0, jnp.maximum(slack, 0))
    shifted = jax.random.randint(jax.random.fold_in(own, 4), (amount // 2,), 0, 1 << 20) % (slack + 1)
    tallies = tallies.at[donor].add(-shifted).at[receiver].add(shifted)
    members = jnp.searchsorted(jnp.cumsum(tallies), jnp.arange(rows * top), side="right").astype(jnp.int32)
    listing = members.reshape(top, rows).T
    listing = listing[jax.random.permutation(jax.random.fold_in(own, 1), rows)]
    rotation = jax.random.randint(jax.random.fold_in(own, 2), (rows, 1), 0, top)
    return jnp.take_along_axis(listing, (jnp.arange(top)[None, :] + rotation) % top, axis=1)


def shares(count, total, most, slope, full):
    loads = [(1 << 20) // math.isqrt(rank ** slope) + 1 for rank in range(1, count + 1)]
    largest = most if full else min(most, max(-(-total // count), total * loads[0] // sum(loads)))
    least = 1 if total - largest >= count - 1 else 0
    given, rest = [largest] + [least] * (count - 1), total - largest - least * (count - 1)
    while rest > 0:
        candidates = [i for i in range(1, count) if given[i] < largest] or [i for i in range(1, count) if given[i] < most]
        mass, left = sum([loads[i] for i in candidates]), rest
        for i in candidates:
            extra = min(most - given[i], max(1, left * loads[i] // mass), rest)
            given[i] = given[i] + extra
            rest = rest - extra
    return np.array(given)


def bell_draw(stream_key, shape, deviation, most, pieces=(), held_as=jnp.bfloat16):
    entries = jax.random.normal(stream_key, shape, jnp.float32) * deviation
    if len(pieces) > 0:
        entries = block_levels(stream_key, shape, pieces, -0.22, 0.18) * entries
    return jnp.clip(entries, min=-most, max=most).astype(held_as)


def setup_inputs(seed: int = 0, part: int = 0) -> dict:
    seeds = jax.random.split(jax.random.key(seed), 12)
    part_keys = jax.random.split(jax.random.fold_in(seeds[11], part), 12)
    latents = bell_draw(part_keys[0], (2, TOKENS, D), 1.0, 6.0, ((0, 2), (1, 16)), jnp.float32)
    modulation = bell_draw(part_keys[1], (2, 6, D), 0.5, 3.0, (), jnp.float32)
    shallow_routes_keys = jax.random.split(jax.random.fold_in(part_keys[2], 1), 2 * TOKENS // TOK_DEV)
    shallow_routes_turns = jax.random.permutation(jax.random.fold_in(part_keys[2], 3), 2 * TOKENS // TOK_DEV)
    shallow_routes = jax.vmap(lambda own, number: routed_block(jax.random.fold_in(part_keys[2], 2), own, number, TOK_DEV, EXPERTS, 2, CAP, 1))(shallow_routes_keys, shallow_routes_turns).reshape((2, TOKENS, 2))
    deep_routes_keys = jax.random.split(jax.random.fold_in(part_keys[3], 1), TOKENS // TOK_DEV)
    deep_routes_turns = jax.random.permutation(jax.random.fold_in(part_keys[3], 3), TOKENS // TOK_DEV)
    deep_routes = jax.vmap(lambda own, number: routed_block(jax.random.fold_in(part_keys[3], 2), own, number, TOK_DEV, EXPERTS, 2, CAP, 1))(deep_routes_keys, deep_routes_turns).reshape((TOKENS, 2))
    refresh = with_ends(jax.random.randint(part_keys[4], (N_EXPERT,), 0, 2), jax.random.fold_in(part_keys[4], 1), 0, 1).astype(jnp.int32)
    shallow_in = bell_draw(seeds[5], (N_EXPERT, D, FF_DEV), D ** -0.5, 0.15625, ((0, 16),))
    shallow_out = bell_draw(seeds[6], (N_EXPERT, FF_DEV, D), FF ** -0.5, 0.109375, ((0, 16),))
    deep_in = bell_draw(seeds[7], (N_EXPERT, D, FF_DEV), D ** -0.5, 0.15625, ((0, 16),))
    deep_out = bell_draw(seeds[8], (N_EXPERT, FF_DEV, D), FF ** -0.5, 0.109375, ((0, 16),))
    shallow_router = bell_draw(seeds[9], (D, EXPERTS), D ** -0.5, 0.15625, (), jnp.float32)
    deep_router = bell_draw(seeds[10], (D, EXPERTS), D ** -0.5, 0.15625, (), jnp.float32)
    return {"latents": latents, "modulation": modulation, "shallow_routes": shallow_routes, "deep_routes": deep_routes, "refresh": refresh, "shallow_in": shallow_in, "shallow_out": shallow_out, "deep_in": deep_in, "deep_out": deep_out, "shallow_router": shallow_router, "deep_router": deep_router}


def modulate(hidden, shift_row, scale_row):
    average = lax.optimization_barrier(jnp.mean(hidden, axis=-1, keepdims=True))
    centred = hidden - average
    variance = lax.optimization_barrier(jnp.mean(centred * centred, axis=-1, keepdims=True))
    return (centred * lax.rsqrt(variance + 1e-06) * (1.0 + scale_row) + shift_row).astype(jnp.bfloat16)

def expert_layer(normed, routes, weight_in, weight_out, router):
    total = normed.shape[0]
    blocks = total // TOK_DEV
    logits = jnp.dot(normed.astype(jnp.float32), router, precision=lax.Precision.HIGHEST)
    chosen = jnp.take_along_axis(logits, routes, axis=1)
    gate_sig = jax.nn.sigmoid(chosen)
    weights = gate_sig / lax.optimization_barrier(jnp.sum(gate_sig, axis=-1, keepdims=True))
    pair_expert = routes.reshape(blocks, TOK_DEV * 2).astype(jnp.int32)
    onehot = (pair_expert[:, :, None] == jnp.arange(EXPERTS, dtype=jnp.int32)).astype(jnp.int32)
    position = lax.optimization_barrier(jnp.sum(onehot * (jnp.cumsum(onehot, axis=1) - 1), axis=-1)).astype(jnp.int32)
    block_ids = jnp.broadcast_to(jnp.arange(blocks, dtype=jnp.int32)[:, None], position.shape)
    token_ids = (jnp.arange(total * 2, dtype=jnp.int32) // 2).reshape(blocks, TOK_DEV * 2)
    slot_table = jnp.full((EXPERTS, blocks, CAP), total, jnp.int32).at[pair_expert, block_ids, position].set(token_ids)
    padded = jnp.concatenate([normed, jnp.zeros((1, D), jnp.bfloat16)], axis=0)

    def one_expert(expert):
        flat_rows = padded[slot_table[expert].reshape(-1)]
        summed = jnp.zeros((blocks * CAP, D), jnp.float32)
        for quarter in range(QUARTERS):
            index = expert * QUARTERS + quarter
            hidden = jax.nn.gelu(jnp.dot(flat_rows, weight_in[index], preferred_element_type=jnp.float32), approximate=True).astype(jnp.bfloat16)
            partial_value = lax.optimization_barrier(jnp.dot(hidden, weight_out[index], preferred_element_type=jnp.float32).astype(jnp.bfloat16))
            summed = summed + partial_value.astype(jnp.float32)
        return summed
    expert_out = lax.map(one_expert, jnp.arange(EXPERTS, dtype=jnp.int32))
    picked = expert_out[pair_expert, block_ids * CAP + position].reshape(total, 2, D)
    return lax.optimization_barrier(jnp.sum(weights[:, :, None] * picked, axis=1))

def reference(latents, modulation, shallow_routes, deep_routes, refresh, shallow_in, shallow_out, deep_in, deep_out, shallow_router, deep_router):
    shallow = []
    for group_idx in range(2):
        normed = modulate(latents[group_idx], modulation[group_idx, 0], modulation[group_idx, 1])
        moe_out = expert_layer(normed, shallow_routes[group_idx], shallow_in, shallow_out, shallow_router)
        shallow.append((latents[group_idx] + modulation[group_idx, 2] * moe_out).astype(jnp.bfloat16))
    after_shallow = jnp.stack(shallow)
    token_root = jnp.repeat(refresh.astype(jnp.int32), TOK_DEV)
    picks_one = (token_root == 1)[:, None]
    chosen_rows = jnp.where(picks_one, after_shallow[1], after_shallow[0])

    def mod_row(index):
        return jnp.where(picks_one, modulation[1, index][None], modulation[0, index][None])
    normed = modulate(chosen_rows.astype(jnp.float32), mod_row(3), mod_row(4))
    moe_out = expert_layer(normed, deep_routes, deep_in, deep_out, deep_router)
    deep_delta = (mod_row(5) * moe_out).astype(jnp.bfloat16)
    return (after_shallow.astype(jnp.float32) + deep_delta.astype(jnp.float32)[None]).astype(jnp.bfloat16)
```

```python
import functools

import jax
import jax.numpy as jnp
from jax import lax
from jax.experimental import pallas as pl
from jax.experimental.pallas import tpu as pltpu
from jax.sharding import PartitionSpec as P

MESH = pl.DeviceIdType.MESH
KINDS = 11
TO_PLANE, TO_X, TO_Y, FWD_Y, FWD_X, BACK_X, BACK_Y, OWN_X, OWN_Y, HOME, SHARE = range(KINDS)


def modulate(hidden, shift_row, scale_row):
    average = jnp.mean(hidden, axis=-1, keepdims=True)
    centred = hidden - average
    variance = jnp.mean(centred * centred, axis=-1, keepdims=True)
    return (centred * lax.rsqrt(variance + 1e-06) * (1.0 + scale_row) + shift_row).astype(
        jnp.bfloat16
    )


def plan(normed, routes, router, capacity, first, count):
    rows_count, width = normed.shape
    experts = router.shape[1]
    logits = jnp.dot(normed.astype(jnp.float32), router, precision=lax.Precision.HIGHEST)
    hits = routes[:, :, None] == jnp.arange(experts, dtype=jnp.int32)
    chosen = jnp.sum(jnp.where(hits, logits[:, None, :], 0.0), axis=-1)
    gate_sig = jax.nn.sigmoid(chosen)
    weights = gate_sig / jnp.sum(gate_sig, axis=-1, keepdims=True)
    named = jnp.any(hits, axis=1)
    earlier = lax.broadcasted_iota(jnp.int32, (rows_count, rows_count), 1) < (
        lax.broadcasted_iota(jnp.int32, (rows_count, rows_count), 0)
    )
    position = jnp.dot(
        earlier.astype(jnp.bfloat16),
        named.astype(jnp.bfloat16),
        preferred_element_type=jnp.float32,
    ).astype(jnp.int32)
    weight_of = jnp.sum(jnp.where(hits, weights[:, :, None], 0.0), axis=1)
    slots = jnp.arange(capacity, dtype=jnp.int32)
    combine_w = jnp.where(
        named[:, :, None] & (position[:, :, None] == slots), weight_of[:, :, None], 0.0
    )
    own_slots = first + jnp.arange(count, dtype=jnp.int32)
    dispatch = (named[:, :, None] & (position[:, :, None] == own_slots)).astype(jnp.bfloat16)
    gathered = jnp.einsum(
        "rs,rd->sd",
        dispatch.reshape(rows_count, experts * count),
        normed,
        preferred_element_type=jnp.float32,
    ).astype(jnp.bfloat16)
    return gathered.reshape(experts, count, width), combine_w


def layer_kernel(
    share,
    tok_ref,
    win_hbm,
    wout_hbm,
    out_ref,
    win,
    wout,
    rows,
    part,
    back_x,
    back_y,
    own_x,
    own_y,
    summed,
    home,
    other,
    w_sem,
    send_sem,
    recv_sem,
):
    experts, cap, width = tok_ref.shape
    half = width // 2
    quarters = lax.axis_size("expert") // experts
    me = lax.axis_index("expert")
    e_me, q_me = me // quarters, me % quarters
    qx, qy = q_me % 2, q_me // 2
    q_x = qy * 2 + (1 - qx)
    q_y = (1 - qy) * 2 + qx
    q_d = (1 - qy) * 2 + (1 - qx)
    dev_x = {"expert": e_me * quarters + q_x}
    dev_y = {"expert": e_me * quarters + q_y}
    sibling = {"step": 1 - lax.axis_index("step")}

    w_copies = [
        pltpu.make_async_copy(win_hbm, win, w_sem.at[0]),
        pltpu.make_async_copy(wout_hbm, wout, w_sem.at[1]),
    ]
    for copy in w_copies:
        copy.start()

    def column(e):
        return {"expert": e * quarters + q_me}

    def ahead(k):
        return (e_me + k) % experts

    def behind(k):
        return (e_me + experts - k) % experts

    barrier = pltpu.get_barrier_semaphore()
    peers = [dev_x, dev_y] + [column(ahead(k)) for k in range(1, experts)]
    if share:
        peers.append(sibling)
    for peer in peers:
        pl.semaphore_signal(barrier, inc=1, device_id=peer, device_id_type=MESH)
    pl.semaphore_wait(barrier, len(peers))

    started = []

    def send(kind, src, dst, device, sent, landed):
        copy = pltpu.make_async_remote_copy(
            src_ref=src,
            dst_ref=dst,
            send_sem=send_sem.at[kind, sent],
            recv_sem=recv_sem.at[kind, landed],
            device_id=device,
            device_id_type=MESH,
        )
        copy.start()
        started.append(copy)

    def arrived(kind, dst, landed):
        pltpu.make_async_remote_copy(
            src_ref=dst,
            dst_ref=dst,
            send_sem=send_sem.at[kind, landed],
            recv_sem=recv_sem.at[kind, landed],
            device_id=dev_x,
            device_id_type=MESH,
        ).wait_recv()

    def at(q):
        return pl.ds(pl.multiple_of(q * cap, cap), cap)

    left, right = pl.ds(0, half), pl.ds(half, half)

    for k in range(1, experts):
        to = ahead(k)
        send(TO_PLANE, tok_ref.at[to], rows.at[e_me, at(q_me)], column(to), to, e_me)
    rows[e_me, at(q_me), :] = tok_ref[e_me]

    def spread(k):
        j = behind(k)
        mine = rows.at[j, at(q_me)]
        if k > 0:
            arrived(TO_PLANE, mine, j)
        send(TO_X, mine, mine, dev_x, j, j)
        send(TO_Y, mine, mine, dev_y, j, j)

    def forward(k):
        j = behind(k)
        arrived(TO_X, rows.at[j, at(q_x)], j)
        block = rows.at[j, at(q_x), left]
        send(FWD_Y, block, block, dev_y, j, j)
        arrived(TO_Y, rows.at[j, at(q_y)], j)
        block = rows.at[j, at(q_y), right]
        send(FWD_X, block, block, dev_x, j, j)

    def compute(k):
        j = behind(k)
        arrived(FWD_Y, rows.at[j, at(q_d), left], j)
        arrived(FWD_X, rows.at[j, at(q_d), right], j)
        if k == 0:
            for copy in w_copies:
                copy.wait()
        hidden = jax.nn.gelu(
            jnp.dot(rows[j], win[...], preferred_element_type=jnp.float32), approximate=True
        ).astype(jnp.bfloat16)
        for columns in (left, right):
            part[j, :, columns] = jnp.dot(
                hidden, wout[:, columns], preferred_element_type=jnp.float32
            ).astype(jnp.bfloat16)
        send(BACK_X, part.at[j, at(q_d), left], back_x.at[j], dev_x, j, j)
        send(BACK_Y, part.at[j, at(q_d), right], back_y.at[j], dev_y, j, j)

    def gather(k):
        j = behind(k)
        arrived(BACK_X, back_x.at[j], j)
        part[j, at(q_y), left] = (
            part[j, at(q_y), left].astype(jnp.float32) + back_x[j].astype(jnp.float32)
        ).astype(jnp.bfloat16)
        send(OWN_Y, part.at[j, at(q_y)], own_y.at[j], dev_y, j, j)
        arrived(BACK_Y, back_y.at[j], j)
        part[j, at(q_x), right] = (
            part[j, at(q_x), right].astype(jnp.float32) + back_y[j].astype(jnp.float32)
        ).astype(jnp.bfloat16)
        send(OWN_X, part.at[j, at(q_x)], own_x.at[j], dev_x, j, j)

    def finish(k):
        j = behind(k)
        arrived(OWN_Y, own_y.at[j], j)
        arrived(OWN_X, own_x.at[j], j)
        total = (
            part[j, at(q_me), :].astype(jnp.float32)
            + own_x[j].astype(jnp.float32)
            + own_y[j].astype(jnp.float32)
        ).astype(jnp.bfloat16)
        if k == 0:
            home[j] = total
            if share:
                send(SHARE, home.at[j], other.at[j], sibling, j, j)
        else:
            summed[j] = total
            send(HOME, summed.at[j], home.at[e_me], column(j), j, e_me)

    stages = (spread, forward, compute, gather, finish)
    for turn in range(experts + len(stages) - 1):
        for lag, stage in enumerate(stages):
            if 0 <= turn - lag < experts:
                stage(turn - lag)

    for k in range(1, experts):
        j = ahead(k)
        arrived(HOME, home.at[j], j)
        if share:
            send(SHARE, home.at[j], other.at[j], sibling, j, j)
    if share:
        core = lax.axis_index("step")
        out_ref[core] = home[...]
        for j in range(experts):
            arrived(SHARE, other.at[j], j)
        out_ref[1 - core] = other[...]
    else:
        out_ref[0] = home[...]
    for copy in started:
        copy.wait_send()


def layer(tokens, weight_in, weight_out, share, collective_id):
    experts, cap, width = tokens.shape
    quarters = lax.axis_size("expert") // experts
    assert quarters == 4
    halves = 2 if share else 1
    bf16 = jnp.bfloat16
    vmem = pl.BlockSpec(memory_space=pltpu.VMEM)
    hbm = pl.BlockSpec(memory_space=pl.ANY)
    block = pltpu.VMEM((experts, cap, width), bf16)
    return pl.pallas_call(
        functools.partial(layer_kernel, share),
        out_shape=jax.ShapeDtypeStruct((halves, experts, cap, width), bf16),
        in_specs=[vmem, hbm, hbm],
        out_specs=vmem,
        scratch_shapes=[
            pltpu.VMEM(weight_in.shape, bf16),
            pltpu.VMEM(weight_out.shape, bf16),
            pltpu.VMEM((experts, quarters * cap, width), bf16),
            pltpu.VMEM((experts, quarters * cap, width), bf16),
            pltpu.VMEM((experts, cap, width // 2), bf16),
            pltpu.VMEM((experts, cap, width // 2), bf16),
            block,
            block,
            block,
            block,
            block,
            pltpu.SemaphoreType.DMA((2,)),
            pltpu.SemaphoreType.DMA((KINDS, experts)),
            pltpu.SemaphoreType.DMA((KINDS, experts)),
        ],
        compiler_params=pltpu.CompilerParams(
            collective_id=collective_id, has_side_effects=True, vmem_limit_bytes=48 * 1024 * 1024
        ),
    )(tokens, weight_in, weight_out)


def combine(returned, combine_w):
    halves, experts, cap, width = returned.shape
    rows_count = combine_w.shape[0]
    ordered = jnp.swapaxes(combine_w.reshape(rows_count, experts, halves, cap), 1, 2)
    return jnp.dot(
        ordered.reshape(rows_count, -1),
        returned.astype(jnp.float32).reshape(-1, width),
        precision=lax.Precision.HIGHEST,
        preferred_element_type=jnp.float32,
    )


def body(
    latents,
    modulation,
    shallow_routes,
    deep_routes,
    refresh,
    shallow_in,
    shallow_out,
    deep_in,
    deep_out,
    shallow_router,
    deep_router,
):
    experts = shallow_router.shape[1]
    rows_count = latents.shape[1]
    capacity = 2 * max(rows_count * 5 // 64, rows_count // experts)
    capacity = -(-capacity // 32) * 32
    step_idx = lax.axis_index("step")
    root_idx = refresh[0]
    own_mod = lax.dynamic_index_in_dim(modulation, step_idx, 0, keepdims=False)
    features = latents[0]
    normed = modulate(features, own_mod[0], own_mod[1])
    gathered, combine_w = plan(normed, shallow_routes[0], shallow_router, capacity, 0, capacity)
    returned = layer(gathered, shallow_in[0], shallow_out[0], False, 0)
    moe_shallow = combine(returned, combine_w)
    after_shallow = (features + own_mod[2] * moe_shallow).astype(jnp.bfloat16)
    normed_deep = modulate(after_shallow.astype(jnp.float32), own_mod[3], own_mod[4])
    from_other = lax.ppermute(normed_deep, "step", [(0, 1), (1, 0)])
    normed_root = jnp.where(root_idx == step_idx, normed_deep, from_other)
    part_cap = capacity // 2
    gathered_deep, combine_deep = plan(
        normed_root, deep_routes, deep_router, capacity, step_idx * part_cap, part_cap
    )
    returned_deep = layer(gathered_deep, deep_in[0], deep_out[0], True, 1)
    moe_deep = combine(returned_deep, combine_deep)
    root_gate = lax.dynamic_index_in_dim(modulation, root_idx, 0, keepdims=False)[5]
    deep_delta = (root_gate * moe_deep).astype(jnp.bfloat16)
    result = (after_shallow.astype(jnp.float32) + deep_delta.astype(jnp.float32)).astype(
        jnp.bfloat16
    )
    return result[None]


def solution(mesh):
    in_specs = (
        P("step", ("group", "expert"), None),
        P("group", None, None),
        P("step", ("group", "expert"), None),
        P(("group", "expert"), None),
        P(("group", "expert")),
        P("expert", None, None),
        P("expert", None, None),
        P("expert", None, None),
        P("expert", None, None),
        P(),
        P(),
    )
    out_specs = P("step", ("group", "expert"), None)
    return jax.shard_map(body, mesh=mesh, in_specs=in_specs, out_specs=out_specs, check_vma=False)
```

```python
import functools

import jax
import jax.numpy as jnp
from jax import lax
from jax.experimental import pallas as pl
from jax.experimental.pallas import tpu as pltpu
from jax.sharding import PartitionSpec as P

MESH = pl.DeviceIdType.MESH
KINDS = 11
TO_PLANE, TO_X, TO_Y, FWD_Y, FWD_X, BACK_X, BACK_Y, OWN_X, OWN_Y, HOME, SHARE = range(KINDS)


def modulate(hidden, shift_row, scale_row):
    average = jnp.mean(hidden, axis=-1, keepdims=True)
    centred = hidden - average
    variance = jnp.mean(centred * centred, axis=-1, keepdims=True)
    return (centred * lax.rsqrt(variance + 1e-06) * (1.0 + scale_row) + shift_row).astype(
        jnp.bfloat16
    )


def plan(normed, routes, router, capacity, first, count):
    rows_count, width = normed.shape
    experts = router.shape[1]
    logits = jnp.dot(normed.astype(jnp.float32), router, precision=lax.Precision.HIGHEST)
    hits = routes[:, :, None] == jnp.arange(experts, dtype=jnp.int32)
    chosen = jnp.sum(jnp.where(hits, logits[:, None, :], 0.0), axis=-1)
    gate_sig = jax.nn.sigmoid(chosen)
    weights = gate_sig / jnp.sum(gate_sig, axis=-1, keepdims=True)
    named = jnp.any(hits, axis=1)
    earlier = lax.broadcasted_iota(jnp.int32, (rows_count, rows_count), 1) < (
        lax.broadcasted_iota(jnp.int32, (rows_count, rows_count), 0)
    )
    position = jnp.dot(
        earlier.astype(jnp.bfloat16),
        named.astype(jnp.bfloat16),
        preferred_element_type=jnp.float32,
    ).astype(jnp.int32)
    weight_of = jnp.sum(jnp.where(hits, weights[:, :, None], 0.0), axis=1)
    slots = jnp.arange(capacity, dtype=jnp.int32)
    combine_w = jnp.where(
        named[:, :, None] & (position[:, :, None] == slots), weight_of[:, :, None], 0.0
    )
    own_slots = first + jnp.arange(count, dtype=jnp.int32)
    dispatch = (named[:, :, None] & (position[:, :, None] == own_slots)).astype(jnp.bfloat16)
    gathered = jnp.einsum(
        "rs,rd->sd",
        dispatch.reshape(rows_count, experts * count),
        normed,
        preferred_element_type=jnp.float32,
    ).astype(jnp.bfloat16)
    return gathered.reshape(experts, count, width), combine_w


def layer_kernel(
    share,
    tok_ref,
    win_hbm,
    wout_hbm,
    out_ref,
    win,
    wout,
    rows,
    part,
    back_x,
    back_y,
    own_x,
    own_y,
    summed,
    home,
    other,
    w_sem,
    send_sem,
    recv_sem,
):
    experts, cap, width = tok_ref.shape
    half = width // 2
    quarters = lax.axis_size("expert") // experts
    me = lax.axis_index("expert")
    e_me, q_me = me // quarters, me % quarters
    qx, qy = q_me % 2, q_me // 2
    q_x = qy * 2 + (1 - qx)
    q_y = (1 - qy) * 2 + qx
    q_d = (1 - qy) * 2 + (1 - qx)
    dev_x = {"expert": e_me * quarters + q_x}
    dev_y = {"expert": e_me * quarters + q_y}
    sibling = {"step": 1 - lax.axis_index("step")}

    w_copies = [
        pltpu.make_async_copy(win_hbm, win, w_sem.at[0]),
        pltpu.make_async_copy(wout_hbm, wout, w_sem.at[1]),
    ]
    for copy in w_copies:
        copy.start()

    def column(e):
        return {"expert": e * quarters + q_me}

    def ahead(k):
        return (e_me + k) % experts

    def behind(k):
        return (e_me + experts - k) % experts

    barrier = pltpu.get_barrier_semaphore()
    peers = [dev_x, dev_y] + [column(ahead(k)) for k in range(1, experts)]
    if share:
        peers.append(sibling)
    for peer in peers:
        pl.semaphore_signal(barrier, inc=1, device_id=peer, device_id_type=MESH)
    pl.semaphore_wait(barrier, len(peers))

    started = []

    def send(kind, src, dst, device, sent, landed):
        copy = pltpu.make_async_remote_copy(
            src_ref=src,
            dst_ref=dst,
            send_sem=send_sem.at[kind, sent],
            recv_sem=recv_sem.at[kind, landed],
            device_id=device,
            device_id_type=MESH,
        )
        copy.start()
        started.append(copy)

    def arrived(kind, dst, landed):
        pltpu.make_async_remote_copy(
            src_ref=dst,
            dst_ref=dst,
            send_sem=send_sem.at[kind, landed],
            recv_sem=recv_sem.at[kind, landed],
            device_id=dev_x,
            device_id_type=MESH,
        ).wait_recv()

    def at(q):
        return pl.ds(pl.multiple_of(q * cap, cap), cap)

    left, right = pl.ds(0, half), pl.ds(half, half)

    for k in range(1, experts):
        to = ahead(k)
        send(TO_PLANE, tok_ref.at[to], rows.at[e_me, at(q_me)], column(to), to, e_me)
    rows[e_me, at(q_me), :] = tok_ref[e_me]

    def spread(k):
        j = behind(k)
        mine = rows.at[j, at(q_me)]
        if k > 0:
            arrived(TO_PLANE, mine, j)
        send(TO_X, mine, mine, dev_x, j, j)
        send(TO_Y, mine, mine, dev_y, j, j)

    def forward(k):
        j = behind(k)
        arrived(TO_X, rows.at[j, at(q_x)], j)
        block = rows.at[j, at(q_x), left]
        send(FWD_Y, block, block, dev_y, j, j)
        arrived(TO_Y, rows.at[j, at(q_y)], j)
        block = rows.at[j, at(q_y), right]
        send(FWD_X, block, block, dev_x, j, j)

    def compute(k):
        j = behind(k)
        arrived(FWD_Y, rows.at[j, at(q_d), left], j)
        arrived(FWD_X, rows.at[j, at(q_d), right], j)
        if k == near_last[0]:
            for copy in w_copies:
                copy.wait()
        hidden = jax.nn.gelu(
            jnp.dot(rows[j], win[...], preferred_element_type=jnp.float32), approximate=True
        ).astype(jnp.bfloat16)
        for columns in (left, right):
            part[j, :, columns] = jnp.dot(
                hidden, wout[:, columns], preferred_element_type=jnp.float32
            ).astype(jnp.bfloat16)
        send(BACK_X, part.at[j, at(q_d), left], back_x.at[j], dev_x, j, j)
        send(BACK_Y, part.at[j, at(q_d), right], back_y.at[j], dev_y, j, j)

    def gather(k):
        j = behind(k)
        arrived(BACK_X, back_x.at[j], j)
        part[j, at(q_y), left] = (
            part[j, at(q_y), left].astype(jnp.float32) + back_x[j].astype(jnp.float32)
        ).astype(jnp.bfloat16)
        send(OWN_Y, part.at[j, at(q_y)], own_y.at[j], dev_y, j, j)
        arrived(BACK_Y, back_y.at[j], j)
        part[j, at(q_x), right] = (
            part[j, at(q_x), right].astype(jnp.float32) + back_y[j].astype(jnp.float32)
        ).astype(jnp.bfloat16)
        send(OWN_X, part.at[j, at(q_x)], own_x.at[j], dev_x, j, j)

    def finish(k):
        j = behind(k)
        arrived(OWN_Y, own_y.at[j], j)
        arrived(OWN_X, own_x.at[j], j)
        total = (
            part[j, at(q_me), :].astype(jnp.float32)
            + own_x[j].astype(jnp.float32)
            + own_y[j].astype(jnp.float32)
        ).astype(jnp.bfloat16)
        if k == 0:
            home[j] = total
            if share:
                send(SHARE, home.at[j], other.at[j], sibling, j, j)
        else:
            summed[j] = total
            send(HOME, summed.at[j], home.at[e_me], column(j), j, e_me)

    def relay(k):
        j = ahead(k)
        arrived(HOME, home.at[j], j)
        if share:
            send(SHARE, home.at[j], other.at[j], sibling, j, j)

    near_first = list(range(experts))
    near_last = near_first[1:] + [0]
    stages = (
        (spread, near_first),
        (forward, near_first),
        (compute, near_last),
        (gather, near_last),
        (finish, near_last),
        (relay, near_last[:-1]),
    )
    for turn in range(experts + len(stages) - 1):
        for lag, (stage, order) in enumerate(stages):
            if 0 <= turn - lag < len(order):
                stage(order[turn - lag])

    if share:
        core = lax.axis_index("step")
        out_ref[core] = home[...]
        for j in range(experts):
            arrived(SHARE, other.at[j], j)
        out_ref[1 - core] = other[...]
    else:
        out_ref[0] = home[...]
    for copy in started:
        copy.wait_send()


def layer(tokens, weight_in, weight_out, share, collective_id):
    experts, cap, width = tokens.shape
    quarters = lax.axis_size("expert") // experts
    assert quarters == 4
    halves = 2 if share else 1
    bf16 = jnp.bfloat16
    vmem = pl.BlockSpec(memory_space=pltpu.VMEM)
    hbm = pl.BlockSpec(memory_space=pl.ANY)
    block = pltpu.VMEM((experts, cap, width), bf16)
    return pl.pallas_call(
        functools.partial(layer_kernel, share),
        out_shape=jax.ShapeDtypeStruct((halves, experts, cap, width), bf16),
        in_specs=[vmem, hbm, hbm],
        out_specs=vmem,
        scratch_shapes=[
            pltpu.VMEM(weight_in.shape, bf16),
            pltpu.VMEM(weight_out.shape, bf16),
            pltpu.VMEM((experts, quarters * cap, width), bf16),
            pltpu.VMEM((experts, quarters * cap, width), bf16),
            pltpu.VMEM((experts, cap, width // 2), bf16),
            pltpu.VMEM((experts, cap, width // 2), bf16),
            block,
            block,
            block,
            block,
            block,
            pltpu.SemaphoreType.DMA((2,)),
            pltpu.SemaphoreType.DMA((KINDS, experts)),
            pltpu.SemaphoreType.DMA((KINDS, experts)),
        ],
        compiler_params=pltpu.CompilerParams(
            collective_id=collective_id, has_side_effects=True, vmem_limit_bytes=48 * 1024 * 1024
        ),
    )(tokens, weight_in, weight_out)


def combine(returned, combine_w):
    halves, experts, cap, width = returned.shape
    rows_count = combine_w.shape[0]
    ordered = jnp.swapaxes(combine_w.reshape(rows_count, experts, halves, cap), 1, 2)
    return jnp.dot(
        ordered.reshape(rows_count, -1),
        returned.astype(jnp.float32).reshape(-1, width),
        precision=lax.Precision.HIGHEST,
        preferred_element_type=jnp.float32,
    )


def body(
    latents,
    modulation,
    shallow_routes,
    deep_routes,
    refresh,
    shallow_in,
    shallow_out,
    deep_in,
    deep_out,
    shallow_router,
    deep_router,
):
    experts = shallow_router.shape[1]
    rows_count = latents.shape[1]
    capacity = 2 * max(rows_count * 5 // 64, rows_count // experts)
    capacity = -(-capacity // 32) * 32
    step_idx = lax.axis_index("step")
    root_idx = refresh[0]
    own_mod = lax.dynamic_index_in_dim(modulation, step_idx, 0, keepdims=False)
    features = latents[0]
    normed = modulate(features, own_mod[0], own_mod[1])
    gathered, combine_w = plan(normed, shallow_routes[0], shallow_router, capacity, 0, capacity)
    returned = layer(gathered, shallow_in[0], shallow_out[0], False, 0)
    moe_shallow = combine(returned, combine_w)
    after_shallow = (features + own_mod[2] * moe_shallow).astype(jnp.bfloat16)
    normed_deep = modulate(after_shallow.astype(jnp.float32), own_mod[3], own_mod[4])
    from_other = lax.ppermute(normed_deep, "step", [(0, 1), (1, 0)])
    normed_root = jnp.where(root_idx == step_idx, normed_deep, from_other)
    part_cap = capacity // 2
    gathered_deep, combine_deep = plan(
        normed_root, deep_routes, deep_router, capacity, step_idx * part_cap, part_cap
    )
    returned_deep = layer(gathered_deep, deep_in[0], deep_out[0], True, 1)
    moe_deep = combine(returned_deep, combine_deep)
    root_gate = lax.dynamic_index_in_dim(modulation, root_idx, 0, keepdims=False)[5]
    deep_delta = (root_gate * moe_deep).astype(jnp.bfloat16)
    result = (after_shallow.astype(jnp.float32) + deep_delta.astype(jnp.float32)).astype(
        jnp.bfloat16
    )
    return result[None]


def solution(mesh):
    in_specs = (
        P("step", ("group", "expert"), None),
        P("group", None, None),
        P("step", ("group", "expert"), None),
        P(("group", "expert"), None),
        P(("group", "expert")),
        P("expert", None, None),
        P("expert", None, None),
        P("expert", None, None),
        P("expert", None, None),
        P(),
        P(),
    )
    out_specs = P("step", ("group", "expert"), None)
    return jax.shard_map(body, mesh=mesh, in_specs=in_specs, out_specs=out_specs, check_vma=False)
```

```python
import functools

import jax
import jax.numpy as jnp
from jax import lax
from jax.experimental import pallas as pl
from jax.experimental.pallas import tpu as pltpu
from jax.sharding import PartitionSpec as P

MESH = pl.DeviceIdType.MESH
KINDS = 11
TO_PLANE, TO_X, TO_Y, FWD_Y, FWD_X, BACK_X, BACK_Y, OWN_X, OWN_Y, HOME, SHARE = range(KINDS)


def modulate(hidden, shift_row, scale_row):
    average = jnp.mean(hidden, axis=-1, keepdims=True)
    centred = hidden - average
    variance = jnp.mean(centred * centred, axis=-1, keepdims=True)
    return (centred * lax.rsqrt(variance + 1e-06) * (1.0 + scale_row) + shift_row).astype(
        jnp.bfloat16
    )


def plan(normed, routes, router, capacity, first, count):
    rows_count, width = normed.shape
    experts = router.shape[1]
    logits = jnp.dot(normed.astype(jnp.float32), router, precision=lax.Precision.HIGHEST)
    hits = routes[:, :, None] == jnp.arange(experts, dtype=jnp.int32)
    chosen = jnp.sum(jnp.where(hits, logits[:, None, :], 0.0), axis=-1)
    gate_sig = jax.nn.sigmoid(chosen)
    weights = gate_sig / jnp.sum(gate_sig, axis=-1, keepdims=True)
    named = jnp.any(hits, axis=1)
    earlier = lax.broadcasted_iota(jnp.int32, (rows_count, rows_count), 1) < (
        lax.broadcasted_iota(jnp.int32, (rows_count, rows_count), 0)
    )
    position = jnp.dot(
        earlier.astype(jnp.bfloat16),
        named.astype(jnp.bfloat16),
        preferred_element_type=jnp.float32,
    ).astype(jnp.int32)
    weight_of = jnp.sum(jnp.where(hits, weights[:, :, None], 0.0), axis=1)
    slots = jnp.arange(capacity, dtype=jnp.int32)
    combine_w = jnp.where(
        named[:, :, None] & (position[:, :, None] == slots), weight_of[:, :, None], 0.0
    )
    own_slots = first + jnp.arange(count, dtype=jnp.int32)
    dispatch = (named[:, :, None] & (position[:, :, None] == own_slots)).astype(jnp.bfloat16)
    gathered = jnp.einsum(
        "rs,rd->sd",
        dispatch.reshape(rows_count, experts * count),
        normed,
        preferred_element_type=jnp.float32,
    ).astype(jnp.bfloat16)
    return gathered.reshape(experts, count, width), combine_w


def layer_kernel(
    share,
    tok_ref,
    win_hbm,
    wout_hbm,
    out_ref,
    win,
    wout,
    rows,
    part,
    back_x,
    back_y,
    own_x,
    own_y,
    summed,
    home,
    other,
    w_sem,
    send_sem,
    recv_sem,
):
    experts, cap, width = tok_ref.shape
    half = width // 2
    quarters = lax.axis_size("expert") // experts
    me = lax.axis_index("expert")
    e_me, q_me = me // quarters, me % quarters
    qx, qy = q_me % 2, q_me // 2
    q_x = qy * 2 + (1 - qx)
    q_y = (1 - qy) * 2 + qx
    q_d = (1 - qy) * 2 + (1 - qx)
    dev_x = {"expert": e_me * quarters + q_x}
    dev_y = {"expert": e_me * quarters + q_y}
    sibling = {"step": 1 - lax.axis_index("step")}

    w_copies = [
        pltpu.make_async_copy(win_hbm, win, w_sem.at[0]),
        pltpu.make_async_copy(wout_hbm, wout, w_sem.at[1]),
    ]
    for copy in w_copies:
        copy.start()

    def column(e):
        return {"expert": e * quarters + q_me}

    def ahead(k):
        return (e_me + k) % experts

    def behind(k):
        return (e_me + experts - k) % experts

    barrier = pltpu.get_barrier_semaphore()
    peers = [dev_x, dev_y] + [column(ahead(k)) for k in range(1, experts)]
    if share:
        peers.append(sibling)
    for peer in peers:
        pl.semaphore_signal(barrier, inc=1, device_id=peer, device_id_type=MESH)
    pl.semaphore_wait(barrier, len(peers))

    started = []

    def send(kind, src, dst, device, sent, landed):
        copy = pltpu.make_async_remote_copy(
            src_ref=src,
            dst_ref=dst,
            send_sem=send_sem.at[kind, sent],
            recv_sem=recv_sem.at[kind, landed],
            device_id=device,
            device_id_type=MESH,
        )
        copy.start()
        started.append(copy)

    def arrived(kind, dst, landed):
        pltpu.make_async_remote_copy(
            src_ref=dst,
            dst_ref=dst,
            send_sem=send_sem.at[kind, landed],
            recv_sem=recv_sem.at[kind, landed],
            device_id=dev_x,
            device_id_type=MESH,
        ).wait_recv()

    def at(q):
        return pl.ds(pl.multiple_of(q * cap, cap), cap)

    left, right = pl.ds(0, half), pl.ds(half, half)

    for k in range(1, experts):
        to = ahead(k)
        send(TO_PLANE, tok_ref.at[to], rows.at[e_me, at(q_me)], column(to), to, e_me)
    rows[e_me, at(q_me), :] = tok_ref[e_me]

    def spread(k):
        j = behind(k)
        mine = rows.at[j, at(q_me)]
        if k > 0:
            arrived(TO_PLANE, mine, j)
        send(TO_X, mine, mine, dev_x, j, j)
        send(TO_Y, mine, mine, dev_y, j, j)

    def forward(k):
        j = behind(k)
        arrived(TO_X, rows.at[j, at(q_x)], j)
        block = rows.at[j, at(q_x), left]
        send(FWD_Y, block, block, dev_y, j, j)
        arrived(TO_Y, rows.at[j, at(q_y)], j)
        block = rows.at[j, at(q_y), right]
        send(FWD_X, block, block, dev_x, j, j)

    def compute(k):
        j = behind(k)
        arrived(FWD_Y, rows.at[j, at(q_d), left], j)
        arrived(FWD_X, rows.at[j, at(q_d), right], j)
        if k == 0:
            for copy in w_copies:
                copy.wait()
        hidden = jax.nn.gelu(
            jnp.dot(rows[j], win[...], preferred_element_type=jnp.float32), approximate=True
        ).astype(jnp.bfloat16)
        for columns in (left, right):
            part[j, :, columns] = jnp.dot(
                hidden, wout[:, columns], preferred_element_type=jnp.float32
            ).astype(jnp.bfloat16)
        send(BACK_X, part.at[j, at(q_d), left], back_x.at[j], dev_x, j, j)
        send(BACK_Y, part.at[j, at(q_d), right], back_y.at[j], dev_y, j, j)

    def gather(k):
        j = behind(k)
        arrived(BACK_X, back_x.at[j], j)
        part[j, at(q_y), left] = (
            part[j, at(q_y), left].astype(jnp.float32) + back_x[j].astype(jnp.float32)
        ).astype(jnp.bfloat16)
        send(OWN_Y, part.at[j, at(q_y)], own_y.at[j], dev_y, j, j)
        arrived(BACK_Y, back_y.at[j], j)
        part[j, at(q_x), right] = (
            part[j, at(q_x), right].astype(jnp.float32) + back_y[j].astype(jnp.float32)
        ).astype(jnp.bfloat16)
        send(OWN_X, part.at[j, at(q_x)], own_x.at[j], dev_x, j, j)

    def finish(k):
        j = behind(k)
        arrived(OWN_Y, own_y.at[j], j)
        arrived(OWN_X, own_x.at[j], j)
        total = (
            part[j, at(q_me), :].astype(jnp.float32)
            + own_x[j].astype(jnp.float32)
            + own_y[j].astype(jnp.float32)
        ).astype(jnp.bfloat16)
        if k == 0:
            home[j] = total
            if share:
                send(SHARE, home.at[j], other.at[j], sibling, j, j)
        else:
            summed[j] = total
            send(HOME, summed.at[j], home.at[e_me], column(j), j, e_me)

    def relay(k):
        j = ahead(k)
        arrived(HOME, home.at[j], j)
        if share:
            send(SHARE, home.at[j], other.at[j], sibling, j, j)

    every = list(range(experts))
    stages = (
        (1, forward, every),
        (0, spread, every),
        (2, compute, every),
        (3, gather, every),
        (4, finish, every),
        (6, relay, every[1:]),
    )
    for turn in range(experts + 5):
        for lag, stage, order in stages:
            if 0 <= turn - lag < len(order):
                stage(order[turn - lag])

    if share:
        core = lax.axis_index("step")
        out_ref[core] = home[...]
        for j in range(experts):
            arrived(SHARE, other.at[j], j)
        out_ref[1 - core] = other[...]
    else:
        out_ref[0] = home[...]
    for copy in started:
        copy.wait_send()


def layer(tokens, weight_in, weight_out, share, collective_id):
    experts, cap, width = tokens.shape
    quarters = lax.axis_size("expert") // experts
    assert quarters == 4
    halves = 2 if share else 1
    bf16 = jnp.bfloat16
    vmem = pl.BlockSpec(memory_space=pltpu.VMEM)
    hbm = pl.BlockSpec(memory_space=pl.ANY)
    block = pltpu.VMEM((experts, cap, width), bf16)
    return pl.pallas_call(
        functools.partial(layer_kernel, share),
        out_shape=jax.ShapeDtypeStruct((halves, experts, cap, width), bf16),
        in_specs=[vmem, hbm, hbm],
        out_specs=vmem,
        scratch_shapes=[
            pltpu.VMEM(weight_in.shape, bf16),
            pltpu.VMEM(weight_out.shape, bf16),
            pltpu.VMEM((experts, quarters * cap, width), bf16),
            pltpu.VMEM((experts, quarters * cap, width), bf16),
            pltpu.VMEM((experts, cap, width // 2), bf16),
            pltpu.VMEM((experts, cap, width // 2), bf16),
            block,
            block,
            block,
            block,
            block,
            pltpu.SemaphoreType.DMA((2,)),
            pltpu.SemaphoreType.DMA((KINDS, experts)),
            pltpu.SemaphoreType.DMA((KINDS, experts)),
        ],
        compiler_params=pltpu.CompilerParams(
            collective_id=collective_id, has_side_effects=True, vmem_limit_bytes=48 * 1024 * 1024
        ),
    )(tokens, weight_in, weight_out)


def combine(returned, combine_w):
    halves, experts, cap, width = returned.shape
    rows_count = combine_w.shape[0]
    ordered = jnp.swapaxes(combine_w.reshape(rows_count, experts, halves, cap), 1, 2)
    return jnp.dot(
        ordered.reshape(rows_count, -1),
        returned.astype(jnp.float32).reshape(-1, width),
        precision=lax.Precision.HIGHEST,
        preferred_element_type=jnp.float32,
    )


def body(
    latents,
    modulation,
    shallow_routes,
    deep_routes,
    refresh,
    shallow_in,
    shallow_out,
    deep_in,
    deep_out,
    shallow_router,
    deep_router,
):
    experts = shallow_router.shape[1]
    rows_count = latents.shape[1]
    capacity = 2 * max(rows_count * 5 // 64, rows_count // experts)
    capacity = -(-capacity // 32) * 32
    step_idx = lax.axis_index("step")
    root_idx = refresh[0]
    own_mod = lax.dynamic_index_in_dim(modulation, step_idx, 0, keepdims=False)
    features = latents[0]
    normed = modulate(features, own_mod[0], own_mod[1])
    gathered, combine_w = plan(normed, shallow_routes[0], shallow_router, capacity, 0, capacity)
    returned = layer(gathered, shallow_in[0], shallow_out[0], False, 0)
    moe_shallow = combine(returned, combine_w)
    after_shallow = (features + own_mod[2] * moe_shallow).astype(jnp.bfloat16)
    normed_deep = modulate(after_shallow.astype(jnp.float32), own_mod[3], own_mod[4])
    from_other = lax.ppermute(normed_deep, "step", [(0, 1), (1, 0)])
    normed_root = jnp.where(root_idx == step_idx, normed_deep, from_other)
    part_cap = capacity // 2
    gathered_deep, combine_deep = plan(
        normed_root, deep_routes, deep_router, capacity, step_idx * part_cap, part_cap
    )
    returned_deep = layer(gathered_deep, deep_in[0], deep_out[0], True, 1)
    moe_deep = combine(returned_deep, combine_deep)
    root_gate = lax.dynamic_index_in_dim(modulation, root_idx, 0, keepdims=False)[5]
    deep_delta = (root_gate * moe_deep).astype(jnp.bfloat16)
    result = (after_shallow.astype(jnp.float32) + deep_delta.astype(jnp.float32)).astype(
        jnp.bfloat16
    )
    return result[None]


def solution(mesh):
    in_specs = (
        P("step", ("group", "expert"), None),
        P("group", None, None),
        P("step", ("group", "expert"), None),
        P(("group", "expert"), None),
        P(("group", "expert")),
        P("expert", None, None),
        P("expert", None, None),
        P("expert", None, None),
        P("expert", None, None),
        P(),
        P(),
    )
    out_specs = P("step", ("group", "expert"), None)
    return jax.shard_map(body, mesh=mesh, in_specs=in_specs, out_specs=out_specs, check_vma=False)
```
